32 devices in a mesh: req: 8 (over z, y), grp: 4 (over x, core).
Axes of the slice: x: 2, y: 2, z: 4, core: 2. Of those that a mesh axis runs over, the one named last changes fastest.
Arguments:
- hidden_in: bfloat16 [16384, 1280], P(('req', 'grp')), may hold values from -28 to 28
- queries: bfloat16 [16384, 1280], P(('req', 'grp')), may hold values from -20 to 20
- projected_keys: bfloat16 [16384, 320], P(('req', 'grp')), may hold values from -20 to 20
- projected_values: bfloat16 [16384, 320], P(('req', 'grp')), may hold values from -6 to 6
- segment: int32 [8, 4, 512], P('req', 'grp'), may hold values from 0 to 511, as said below
- live_rows: int32 [8, 4], P('req', 'grp'), may hold values from 0 to 512, as said below
- out_weight: bfloat16 [1280, 1280], replicated, may hold values from -0.15625 to 0.15625
- norm_gain: float32 [1280], replicated, may hold values from 0.5 to 1.5
- gate_weight: bfloat16 [1280, 3584], P(None, 'grp'), may hold values from -0.15625 to 0.15625
- up_weight: bfloat16 [1280, 3584], P(None, 'grp'), may hold values from -0.15625 to 0.15625
- down_weight: bfloat16 [3584, 1280], P('grp'), may hold values from -0.09375 to 0.09375
Outputs:
- layer_out: bfloat16 [16384, 1280], P(('req', 'grp'))
The draws below stay inside these ranges and needn't reach their ends.
Inputs may be any that keep to these rules, and one draw needn't show every extreme that they name: `live_rows`: in each group (one index of grp) the live rows of the 8 owners sum to exactly 1024, and one owner of each group has all 512 slots live. `segment`: within one owner the ids start at 0 at its first slot and rise by 0 or 1 from slot to slot.
All inputs are finite; a program needn't handle non-finite values.
Results may differ from the reference program's by a relative error of at most 0.008.
Values may be sent and summed in bfloat16 or wider, within the bound.
A program may use at most 128 MiB of HBM per device.

```python
import math
import jax
import jax.numpy as jnp
from jax import lax

D = 1280
QUERY_HEADS = 20
KEY_VALUE_HEADS = 5
HEAD_SIZE = 64
FF = 3584
WINDOW = 128
SINK = 4
BAL = 128
OWNER_SLOTS = 512
TOTAL_SLOTS = 16384
N_REQ = 8
N_GRP = 4


def unmasked_field(key, shape):
    visible_field = jnp.clip(jax.random.normal(key, shape, jnp.float32), -4.5, 4.5)
    return visible_field


def draw_queries(key, part):
    visible_field = unmasked_field(jax.random.fold_in(key, 21), (TOTAL_SLOTS, QUERY_HEADS, HEAD_SIZE))
    return visible_field.reshape(TOTAL_SLOTS, QUERY_HEADS * HEAD_SIZE).astype(jnp.bfloat16)


def draw_projected_keys(key, part):
    visible_field = unmasked_field(jax.random.fold_in(key, 22), (TOTAL_SLOTS, KEY_VALUE_HEADS, HEAD_SIZE))
    return visible_field.reshape(TOTAL_SLOTS, KEY_VALUE_HEADS * HEAD_SIZE).astype(jnp.bfloat16)


def draw_hidden_in(key, part):
    first = jax.random.fold_in(jax.random.fold_in(key, 31), 0)
    visible_field = jnp.clip(jax.random.normal(first, (TOTAL_SLOTS, D), jnp.float32), -4.5, 4.5)
    return visible_field.astype(jnp.bfloat16)


def draw_segment(key, part):
    first, second, third, fourth = jax.random.split(jax.random.fold_in(key, 41), 4)
    periods = jnp.array([4, 32, 4096], dtype=jnp.int32)
    choose = jax.random.randint(first, (N_REQ, N_GRP, 1), 0, 3)
    period = jnp.sum(jnp.where(choose == jnp.arange(3, dtype=jnp.int32), periods, 0), axis=-1, keepdims=True)
    draws = jax.random.randint(second, (N_REQ, N_GRP, OWNER_SLOTS), 0, 1 << 30)
    flags = draws % period == 0
    flags = flags | (jnp.arange(OWNER_SLOTS, dtype=jnp.int32) == 0)[None, None, :]
    single_req = jax.random.randint(third, (), 0, N_REQ)
    single_grp = jax.random.randint(fourth, (), 0, N_GRP)
    req_ids = jnp.arange(N_REQ, dtype=jnp.int32)[:, None, None]
    grp_ids = jnp.arange(N_GRP, dtype=jnp.int32)[None, :, None]
    singles = (req_ids == single_req) & (grp_ids == single_grp)
    flags = flags | singles
    return (jnp.cumsum(flags.astype(jnp.int32), axis=-1) - 1).astype(jnp.int32)


def draw_live_rows(key, part):
    first, second, third = jax.random.split(jax.random.fold_in(key, 51), 3)
    quads = N_REQ // 4
    cuts = jnp.sort(jax.random.randint(first, (N_GRP, quads, 3), 0, 4 * BAL + 1), axis=-1)
    lower = jnp.zeros((N_GRP, quads, 1), jnp.int32)
    upper = jnp.full((N_GRP, quads, 1), 4 * BAL, jnp.int32)
    edges = jnp.concatenate([lower, cuts.astype(jnp.int32), upper], axis=-1)
    shares = edges[..., 1:] - edges[..., :-1]
    full_quad = jax.random.randint(second, (N_GRP, 1, 1), 0, quads)
    single = jnp.where(jnp.arange(4, dtype=jnp.int32) == 0, OWNER_SLOTS, 0).astype(jnp.int32)
    shares = jnp.where(jnp.arange(quads, dtype=jnp.int32)[None, :, None] == full_quad, single[None, None, :], shares)
    flat = shares.reshape(N_GRP, N_REQ)

    def shuffle(one_key):
        return jax.random.permutation(one_key, N_REQ)
    orders = jax.vmap(shuffle)(jax.random.split(third, N_GRP))
    placed = jnp.take_along_axis(flat, orders.astype(jnp.int32), axis=1)
    return jnp.transpose(placed).astype(jnp.int32)


def steps_of(key, shape, cuts, least, high):
    factor_of, own = 1.0, jax.random.fold_in(key, 6)
    for dim, parts in cuts:
        steps = jnp.exp(jax.random.uniform(jax.random.fold_in(own, dim), (parts,), jnp.float32, least / len(cuts), high / len(cuts)))
        factor_of = factor_of * jnp.repeat(steps, shape[dim] // parts).reshape([-1 if axis == dim else 1 for axis in range(len(shape))])
    return factor_of


def bell_draw(key, shape, scale, limit, shards=(), kind=jnp.bfloat16):
    level = steps_of(key, shape, shards, -0.22, 0.18) if shards else 1.0
    entries = jax.random.normal(key, shape, jnp.float32) * scale * level
    return jnp.minimum(jnp.maximum(entries, -limit), limit).astype(kind)


def setup_inputs(seed: int = 0) -> dict:
    key_list = jax.random.split(jax.random.key(seed), 12)
    return {
        "hidden_in": draw_hidden_in(jax.random.fold_in(key_list[11], 71), 0),
        "queries": draw_queries(jax.random.fold_in(key_list[11], 71), 0),
        "projected_keys": draw_projected_keys(jax.random.fold_in(key_list[11], 71), 0),
        "projected_values": bell_draw(key_list[3], (TOTAL_SLOTS, KEY_VALUE_HEADS * HEAD_SIZE), 1.0, 6.0, ((0, 32),)),
        "segment": draw_segment(jax.random.fold_in(key_list[11], 71), 0),
        "live_rows": draw_live_rows(jax.random.fold_in(key_list[11], 71), 0),
        "out_weight": bell_draw(key_list[6], (D, D), D ** -0.5, 0.15625),
        "norm_gain": jnp.clip(1.0 + 0.1 * jax.random.normal(key_list[7], (D,), jnp.float32), 0.5, 1.5),
        "gate_weight": bell_draw(key_list[8], (D, FF), D ** -0.5, 0.15625, ((1, 4),)),
        "up_weight": bell_draw(key_list[9], (D, FF), D ** -0.5, 0.15625, ((1, 4),)),
        "down_weight": bell_draw(key_list[10], (FF, D), FF ** -0.5, 0.09375, ((0, 4),)),
    }


rope_base = 10000.0
norm_eps = 1e-05

def apply_rotary(table, token_position):
    half = table.shape[-1] // 2
    inverse = rope_base ** (-(2.0 * jnp.arange(half, dtype=jnp.float32)) / table.shape[-1])
    angle = token_position.astype(jnp.float32)[:, None] * inverse[None, :]
    cosine = jnp.concatenate([jnp.cos(angle), jnp.cos(angle)], axis=-1)[:, None, :]
    sine = jnp.concatenate([jnp.sin(angle), jnp.sin(angle)], axis=-1)[:, None, :]
    numbers = table.astype(jnp.float32)
    turned = jnp.concatenate([-numbers[..., half:], numbers[..., :half]], axis=-1)
    return numbers * cosine + turned * sine

def attend(queries, projected_keys, projected_values, segment):
    slot_capacity = queries.shape[0]
    slots = jnp.arange(slot_capacity, dtype=jnp.int32)
    begins = jnp.concatenate([jnp.ones((1,), dtype=jnp.bool_), segment[1:] != segment[:-1]])
    starts = lax.cummax(jnp.where(begins, slots, 0).astype(jnp.int32), axis=0)
    token_position = slots - starts
    head_group = QUERY_HEADS // KEY_VALUE_HEADS
    query_rotated = apply_rotary(queries.reshape(slot_capacity, QUERY_HEADS, HEAD_SIZE), token_position).astype(jnp.bfloat16).reshape(slot_capacity, KEY_VALUE_HEADS, head_group, HEAD_SIZE)
    key_rotated = apply_rotary(projected_keys.reshape(slot_capacity, KEY_VALUE_HEADS, HEAD_SIZE), token_position).astype(jnp.bfloat16)
    scores = jnp.einsum('qngd,knd->ngqk', query_rotated.astype(jnp.float32), key_rotated.astype(jnp.float32)) / math.sqrt(HEAD_SIZE)
    allowed = (segment[:, None] == segment[None, :]) & (slots[None, :] <= slots[:, None])
    allowed = allowed & ((slots[:, None] - slots[None, :] < WINDOW) | (token_position[None, :] < SINK))
    scores = jnp.where(allowed, scores, -jnp.inf)
    largest = lax.optimization_barrier(jnp.max(scores, axis=-1, keepdims=True))
    raised = jnp.exp(scores - largest)
    layer_weights = (raised / lax.optimization_barrier(jnp.sum(raised, axis=-1, keepdims=True))).astype(jnp.bfloat16)
    attended_context = jnp.einsum('hemz,zhc->mhec', layer_weights.astype(jnp.float32), projected_values.reshape(slot_capacity, KEY_VALUE_HEADS, HEAD_SIZE).astype(jnp.float32))
    return attended_context.reshape(slot_capacity, QUERY_HEADS * HEAD_SIZE).astype(jnp.bfloat16)

def normalize(rows, norm_gain):
    numbers = rows.astype(jnp.float32)
    factor = lax.rsqrt(lax.optimization_barrier(jnp.mean(numbers * numbers, axis=-1, keepdims=True)) + norm_eps)
    return (numbers * factor * norm_gain.astype(jnp.float32)[None, :]).astype(jnp.bfloat16)

def reference(hidden_in, queries, projected_keys, projected_values, segment, live_rows, out_weight, norm_gain, gate_weight, up_weight, down_weight):
    request_owners = N_REQ * N_GRP

    def single_owner(pieces):
        return attend(pieces[0], pieces[1], pieces[2], pieces[3])
    attended_context = lax.map(single_owner, (queries.reshape(request_owners, OWNER_SLOTS, QUERY_HEADS * HEAD_SIZE), projected_keys.reshape(request_owners, OWNER_SLOTS, KEY_VALUE_HEADS * HEAD_SIZE), projected_values.reshape(request_owners, OWNER_SLOTS, KEY_VALUE_HEADS * HEAD_SIZE), segment.reshape(request_owners, OWNER_SLOTS)))
    attended_context = attended_context.reshape(TOTAL_SLOTS, QUERY_HEADS * HEAD_SIZE)
    mixed = (hidden_in.astype(jnp.float32) + jnp.dot(attended_context, out_weight, preferred_element_type=jnp.float32)).astype(jnp.bfloat16)
    keep = (jnp.arange(OWNER_SLOTS, dtype=jnp.int32)[None, :] < live_rows.reshape(request_owners, 1)).reshape(TOTAL_SLOTS)
    order = jnp.argsort(jnp.where(keep, 0, 1).astype(jnp.int32), stable=True).astype(jnp.int32)[:BAL * request_owners]
    rows = mixed[order]
    normed = normalize(rows, norm_gain)
    gate = jnp.dot(normed, gate_weight, preferred_element_type=jnp.float32)
    upward = jnp.dot(normed, up_weight, preferred_element_type=jnp.float32)
    hidden = (jax.nn.silu(gate) * upward).astype(jnp.bfloat16)
    width = FF // N_GRP
    total = jnp.zeros((BAL * request_owners, D), jnp.float32)
    for block in range(N_GRP):
        term = jnp.dot(hidden[:, block * width:(block + 1) * width], down_weight[block * width:(block + 1) * width], preferred_element_type=jnp.float32)
        total = total + lax.optimization_barrier(term.astype(jnp.bfloat16)).astype(jnp.float32)
    result = (rows.astype(jnp.float32) + total).astype(jnp.bfloat16)
    return jnp.zeros((TOTAL_SLOTS, D), jnp.bfloat16).at[order].set(result)
```

```python
import functools

import jax
import jax.numpy as jnp
import numpy as np
from jax import lax
from jax.experimental import pallas as pl
from jax.experimental.pallas import tpu as pltpu
from jax.sharding import PartitionSpec as P

QUERY_HEADS = 20
KEY_VALUE_HEADS = 5
HEAD_SIZE = 64
WINDOW = 128
SINK = 4
ROPE_BASE = 10000.0
NORM_EPS = 1e-05

MESH = pl.DeviceIdType.MESH
F32 = jnp.float32
BF16 = jnp.bfloat16
ROWS = 128
LANES = 256
HEAD_GROUP = QUERY_HEADS // KEY_VALUE_HEADS
HIDDEN_TILE = 128
MASKED = -1e30

CORE, ACROSS, FORWARD, SUM_OWN, SUM_DIAG, SUM_ACROSS = range(6)


def rotary_table(slot_capacity):
    half = HEAD_SIZE // 2
    inverse = np.float32(ROPE_BASE) ** (-(2.0 * np.arange(half, dtype=np.float32)) / HEAD_SIZE)
    angle = np.arange(slot_capacity, dtype=np.float32)[:, None] * inverse.astype(np.float32)[None, :]
    cosine = np.tile(np.cos(angle.astype(np.float64)), (1, 4))
    sine = np.tile(np.sin(angle.astype(np.float64)), (1, 4))
    exact = np.concatenate([cosine, sine], axis=1).astype(np.float32)
    terms = []
    for _ in range(3):
        term = exact.astype(jnp.bfloat16)
        terms.append(term)
        exact = exact - term.astype(np.float32)
    return np.concatenate(terms, axis=1)


def dot(a, b):
    return jnp.dot(a, b, preferred_element_type=F32)


def dot_t(a, b):
    return lax.dot_general(a, b, (((1,), (1,)), ((), ())), preferred_element_type=F32)


def kernel(
    blocks,
    live_ref, queries, keys, values, seg_row, seg_col, table, gain, hidden_hbm, ow_hbm, gate_hbm, up_hbm, down_hbm,
    out,
    hidden, ow, wgu, wd, rows, context, turned_keys, wide_values, cosine, sine, mixed, act, part, own,
    own_out, own_in, diag_out, diag_in, across_out, across_in,
    load_sem, send_sem, recv_sem,
):
    me = lax.axis_index("grp")
    sibling = me + 1 - 2 * lax.rem(me, 2)
    partner = lax.rem(me + 2, 4)
    slots = blocks * ROWS
    tiles = ow.shape[0]
    hidden_tiles = wgu.shape[0]

    loads = []

    def load(src, dst):
        copy = pltpu.make_async_copy(src, dst, load_sem.at[len(loads)])
        copy.start()
        loads.append(copy)
        return copy

    ow_loads = [load(ow_hbm.at[:, pl.ds(LANES * t, LANES)], ow.at[t]) for t in range(tiles)]
    ow_loads.append(load(hidden_hbm, hidden))
    ffn_loads = []
    for t in range(hidden_tiles):
        cols = pl.ds(HIDDEN_TILE * t, HIDDEN_TILE)
        ffn_loads.append(load(gate_hbm.at[:, cols], wgu.at[t, :, pl.ds(0, HIDDEN_TILE)]))
        ffn_loads.append(load(up_hbm.at[:, cols], wgu.at[t, :, pl.ds(HIDDEN_TILE, HIDDEN_TILE)]))
    for t in range(tiles):
        ffn_loads.append(load(down_hbm.at[:, pl.ds(LANES * t, LANES)], wd.at[t]))

    barrier = pltpu.get_barrier_semaphore()
    for other in (sibling, partner):
        pl.semaphore_signal(barrier, inc=1, device_id={"grp": other}, device_id_type=MESH)

    def remote(kind, k, src, dst, other):
        return pltpu.make_async_remote_copy(
            src_ref=src, dst_ref=dst, send_sem=send_sem.at[kind, k], recv_sem=recv_sem.at[kind, k],
            device_id={"grp": other}, device_id_type=MESH,
        )

    to_sibling = [remote(CORE, k, rows.at[k, 0], rows.at[k, 1], sibling) for k in range(blocks)]
    to_partner = [remote(ACROSS, k, rows.at[k, 0], rows.at[k, 2], partner) for k in range(blocks)]
    forward = [remote(FORWARD, k, rows.at[k, 2], rows.at[k, 3], sibling) for k in range(blocks)]
    sum_own = [remote(SUM_OWN, k, own_out.at[k], own_in.at[k], sibling) for k in range(blocks)]
    sum_diag = [remote(SUM_DIAG, k, diag_out.at[k], diag_in.at[k], sibling) for k in range(blocks)]
    sum_across = [remote(SUM_ACROSS, k, across_out.at[k], across_in.at[k], partner) for k in range(blocks)]

    same = seg_col[...] == seg_row[...]
    row_ids = lax.broadcasted_iota(jnp.int32, (slots, slots), 0)
    col_ids = lax.broadcasted_iota(jnp.int32, (slots, slots), 1)
    position = jnp.sum(jnp.where(same & (col_ids <= row_ids), 1.0, 0.0), axis=1, keepdims=True) - 1.0
    key_position = jnp.sum(jnp.where(same & (row_ids <= col_ids), 1.0, 0.0), axis=0, keepdims=True) - 1.0
    chosen = jnp.where(position == col_ids.astype(F32), 1.0, 0.0).astype(BF16)
    factors = dot(chosen, table[...])
    factors = factors[:, :256] + (factors[:, 256:512] + factors[:, 512:])
    cosine[...] = factors[:, :128]
    sine[...] = factors[:, 128:]

    swap_i = lax.broadcasted_iota(jnp.int32, (256, 256), 0)
    swap_j = lax.broadcasted_iota(jnp.int32, (256, 256), 1)
    low = lax.rem(swap_j, HEAD_SIZE) < HEAD_SIZE // 2
    swap = jnp.where(low & (swap_i == swap_j + 32), -1.0, jnp.where(~low & (swap_i == swap_j - 32), 1.0, 0.0))
    swap = swap.astype(BF16)

    key_head = keys[:, :256]
    key_cos, key_sin = cosine[...], sine[...]
    wide_cos = jnp.concatenate([key_cos, key_cos], axis=1)
    wide_sin = jnp.concatenate([key_sin, key_sin], axis=1)
    first = (key_head.astype(F32) * wide_cos + dot(key_head, swap) * wide_sin).astype(BF16)
    key_tail = keys[:, 256:]
    tail = (key_tail.astype(F32) * key_cos[:, :64] + dot(key_tail, swap[:64, :64]) * key_sin[:, :64]).astype(BF16)
    ones = jnp.ones((slots, HEAD_SIZE), BF16)
    for n in range(KEY_VALUE_HEADS):
        turned_keys[n] = first[:, 64 * n : 64 * n + 64] if n < 4 else tail
        wide_values[n] = jnp.concatenate([values[:, 64 * n : 64 * n + 64], ones], axis=1)

    def attend(k):
        lo, width = k * ROWS, (k + 1) * ROWS
        block = pl.ds(lo, ROWS)
        q_ids = lax.broadcasted_iota(jnp.int32, (ROWS, width), 0) + lo
        k_ids = lax.broadcasted_iota(jnp.int32, (ROWS, width), 1)
        allowed = (seg_col[block, :] == seg_row[:, :width]) & (k_ids <= q_ids)
        allowed = allowed & ((q_ids - k_ids < WINDOW) | (key_position[:, :width] < SINK))
        bias = jnp.where(allowed, 0.0, MASKED)
        cos_block, sin_block = cosine[block, :], sine[block, :]
        cos_block = jnp.concatenate([cos_block, cos_block], axis=1)
        sin_block = jnp.concatenate([sin_block, sin_block], axis=1)
        for n in range(KEY_VALUE_HEADS):
            q = queries[block, pl.ds(256 * n, 256)]
            q = (q.astype(F32) * cos_block + dot(q, swap) * sin_block).astype(BF16) * BF16(HEAD_SIZE**-0.5)
            q = jnp.concatenate([q[:, 64 * h : 64 * h + 64] for h in range(HEAD_GROUP)], axis=0)
            scores = dot_t(q, turned_keys[n, :width, :])
            scores = scores.reshape(HEAD_GROUP, ROWS, width) + bias[None]
            raised = jnp.exp(scores - jnp.max(scores, axis=-1, keepdims=True))
            raised = raised.reshape(HEAD_GROUP * ROWS, width).astype(BF16)
            result = dot(raised, wide_values[n, :width, :])
            result = result[:, :64] / result[:, 64:]
            context[:, 256 * n : 256 * n + 256] = jnp.concatenate(
                [result[ROWS * h : ROWS * h + ROWS] for h in range(HEAD_GROUP)], axis=1
            ).astype(BF16)

    def project(k):
        block = pl.ds(k * ROWS, ROWS)
        for t in range(tiles):
            cols = pl.ds(LANES * t, LANES)
            mixed[block, cols] = (hidden[block, cols].astype(F32) + dot(context[...], ow[t])).astype(BF16)
        numbers = mixed[block, :].astype(F32)
        factor = lax.rsqrt(jnp.mean(numbers * numbers, axis=-1, keepdims=True) + NORM_EPS)
        rows[k, 0] = (numbers * factor * gain[...]).astype(BF16)

    def feed_forward(k, first_slot):
        def upward(t, carry):
            both = rows[k, first_slot : first_slot + 2].reshape(2 * ROWS, rows.shape[3])
            product = dot(both, wgu[t])
            gate, up = product[:, :HIDDEN_TILE], product[:, HIDDEN_TILE:]
            act[t] = (gate / (1.0 + jnp.exp(-gate)) * up).astype(BF16)
            return carry

        lax.fori_loop(0, hidden_tiles, upward, 0)
        for t in range(tiles):
            hid = jnp.concatenate([act[j] for j in range(hidden_tiles)], axis=1)
            part[:, LANES * t : LANES * t + LANES] = dot(hid, wd[t])

    def start_block(k):
        attend(k)
        if k == 0:
            for copy in ow_loads:
                copy.wait()
        project(k)
        if k == 0:
            pl.semaphore_wait(barrier, 2)
        to_partner[k].start()
        to_sibling[k].start()

    start_block(0)
    for k in range(blocks):
        if k + 1 < blocks:
            start_block(k + 1)
        if k == 0:
            for copy in ffn_loads:
                copy.wait()
        to_sibling[k].wait_recv()
        feed_forward(k, 0)
        own[k] = part[:ROWS, :]
        own_out[k] = part[ROWS:, :].astype(BF16)
        sum_own[k].start()
        to_partner[k].wait_recv()
        forward[k].start()
        forward[k].wait_recv()
        feed_forward(k, 2)
        diag_out[k] = part[ROWS:, :].astype(BF16)
        sum_diag[k].start()
        sum_diag[k].wait_recv()
        across_out[k] = (part[:ROWS, :] + diag_in[k].astype(F32)).astype(BF16)
        sum_across[k].start()

    live = live_ref[0, 0]
    for k in range(blocks):
        sum_own[k].wait_recv()
        sum_across[k].wait_recv()
        block = pl.ds(k * ROWS, ROWS)
        total = own[k] + own_in[k].astype(F32) + across_in[k].astype(F32) + mixed[block, :].astype(F32)
        slot = lax.broadcasted_iota(jnp.int32, total.shape, 0) + k * ROWS
        out[block, :] = jnp.where(slot < live, total, 0.0).astype(BF16)
    for k in range(blocks):
        for copy in (to_sibling[k], to_partner[k], forward[k], sum_own[k], sum_diag[k], sum_across[k]):
            copy.wait_send()


def on_device(
    hidden_in, queries, projected_keys, projected_values, segment, live_rows, out_weight, norm_gain,
    gate_weight, up_weight, down_weight,
):
    slots, width = hidden_in.shape
    units = gate_weight.shape[1]
    blocks, tiles, hidden_tiles = slots // ROWS, width // LANES, units // HIDDEN_TILE
    vmem = pl.BlockSpec(memory_space=pltpu.VMEM)
    hbm = pl.BlockSpec(memory_space=pl.ANY)
    block_bf16 = pltpu.VMEM((blocks, ROWS, width), BF16)
    return pl.pallas_call(
        functools.partial(kernel, blocks),
        out_shape=jax.ShapeDtypeStruct((slots, width), BF16),
        in_specs=[pl.BlockSpec(memory_space=pltpu.SMEM)] + [vmem] * 7 + [hbm] * 5,
        out_specs=vmem,
        scratch_shapes=[
            pltpu.VMEM((slots, width), BF16),
            pltpu.VMEM((tiles, width, LANES), BF16),
            pltpu.VMEM((hidden_tiles, width, 2 * HIDDEN_TILE), BF16),
            pltpu.VMEM((tiles, units, LANES), BF16),
            pltpu.VMEM((blocks, 4, ROWS, width), BF16),
            pltpu.VMEM((ROWS, width), BF16),
            pltpu.VMEM((KEY_VALUE_HEADS, slots, HEAD_SIZE), BF16),
            pltpu.VMEM((KEY_VALUE_HEADS, slots, 2 * HEAD_SIZE), BF16),
            pltpu.VMEM((slots, 128), F32),
            pltpu.VMEM((slots, 128), F32),
            pltpu.VMEM((slots, width), BF16),
            pltpu.VMEM((hidden_tiles, 2 * ROWS, HIDDEN_TILE), BF16),
            pltpu.VMEM((2 * ROWS, width), F32),
            pltpu.VMEM((blocks, ROWS, width), F32),
            block_bf16, block_bf16, block_bf16, block_bf16, block_bf16, block_bf16,
            pltpu.SemaphoreType.DMA((2 * tiles + 2 * hidden_tiles + 1,)),
            pltpu.SemaphoreType.DMA((6, blocks)),
            pltpu.SemaphoreType.DMA((6, blocks)),
        ],
        compiler_params=pltpu.CompilerParams(
            collective_id=0, has_side_effects=True, vmem_limit_bytes=56 * 1024 * 1024
        ),
        name="decoder_layer",
    )(
        live_rows,
        queries,
        projected_keys,
        projected_values,
        segment.reshape(1, slots),
        segment.reshape(slots, 1),
        jnp.asarray(rotary_table(slots)),
        norm_gain.reshape(1, width),
        hidden_in,
        out_weight,
        gate_weight,
        up_weight,
        down_weight,
    )


def solution(mesh):
    placed = (
        P(("req", "grp"), None),
        P(("req", "grp"), None),
        P(("req", "grp"), None),
        P(("req", "grp"), None),
        P("req", "grp", None),
        P("req", "grp"),
        P(),
        P(),
        P(None, "grp"),
        P(None, "grp"),
        P("grp", None),
    )
    return jax.shard_map(
        on_device, mesh=mesh, in_specs=placed, out_specs=P(("req", "grp"), None), check_vma=False
    )
```

```python
import functools

import jax
import jax.numpy as jnp
import numpy as np
from jax import lax
from jax.experimental import pallas as pl
from jax.experimental.pallas import tpu as pltpu
from jax.sharding import PartitionSpec as P

QUERY_HEADS = 20
KEY_VALUE_HEADS = 5
HEAD_SIZE = 64
WINDOW = 128
SINK = 4
ROPE_BASE = 10000.0
NORM_EPS = 1e-05

MESH = pl.DeviceIdType.MESH
F32 = jnp.float32
BF16 = jnp.bfloat16
ROWS = 128
LANES = 256
HEAD_GROUP = QUERY_HEADS // KEY_VALUE_HEADS
HIDDEN_TILE = 128
MASKED = -1e30

CORE, ACROSS, FORWARD, SUM_OWN, SUM_DIAG, SUM_ACROSS = range(6)


def rotary_table(slot_capacity):
    half = HEAD_SIZE // 2
    inverse = np.float32(ROPE_BASE) ** (-(2.0 * np.arange(half, dtype=np.float32)) / HEAD_SIZE)
    angle = np.arange(slot_capacity, dtype=np.float32)[:, None] * inverse.astype(np.float32)[None, :]
    cosine = np.tile(np.cos(angle.astype(np.float64)), (1, 4))
    sine = np.tile(np.sin(angle.astype(np.float64)), (1, 4))
    exact = np.concatenate([cosine, sine], axis=1).astype(np.float32)
    terms = []
    for _ in range(3):
        term = exact.astype(jnp.bfloat16)
        terms.append(term)
        exact = exact - term.astype(np.float32)
    turned = np.concatenate([np.concatenate([term[:, :half], term[:, 128 : 128 + half]], axis=1).T for term in terms])
    return np.concatenate(terms, axis=1), turned


def dot(a, b):
    return jnp.dot(a, b, preferred_element_type=F32)


def dot_t(a, b):
    return lax.dot_general(a, b, (((1,), (1,)), ((), ())), preferred_element_type=F32)


def kernel(
    blocks,
    live_ref, queries, keys, values, seg_row, table, turned_table, gain, hidden_hbm, ow_hbm, gate_hbm, up_hbm, down_hbm,
    out,
    hidden, ow, wgu, wd, rows, context, turned_keys, wide_values, mixed, finished, act, part, own,
    own_out, own_in, diag_out, diag_in, across_out, across_in,
    load_sem, send_sem, recv_sem, store_sem,
):
    me = lax.axis_index("grp")
    sibling = me + 1 - 2 * lax.rem(me, 2)
    partner = lax.rem(me + 2, 4)
    slots = blocks * ROWS
    tiles = ow.shape[0]
    hidden_tiles = wgu.shape[0]

    loads = []

    def load(src, dst):
        copy = pltpu.make_async_copy(src, dst, load_sem.at[len(loads)])
        copy.start()
        loads.append(copy)
        return copy

    ow_loads = [load(ow_hbm.at[:, pl.ds(LANES * t, LANES)], ow.at[t]) for t in range(tiles)]
    ow_loads.append(load(hidden_hbm, hidden))
    ffn_loads = []

    barrier = pltpu.get_barrier_semaphore()
    for other in (sibling, partner):
        pl.semaphore_signal(barrier, inc=1, device_id={"grp": other}, device_id_type=MESH)

    def remote(kind, k, src, dst, other):
        return pltpu.make_async_remote_copy(
            src_ref=src, dst_ref=dst, send_sem=send_sem.at[kind, k], recv_sem=recv_sem.at[kind, k],
            device_id={"grp": other}, device_id_type=MESH,
        )

    to_sibling = [remote(CORE, k, rows.at[k, 0], rows.at[k, 1], sibling) for k in range(blocks)]
    to_partner = [remote(ACROSS, k, rows.at[k, 0], rows.at[k, 2], partner) for k in range(blocks)]
    forward = [remote(FORWARD, k, rows.at[k, 2], rows.at[k, 3], sibling) for k in range(blocks)]
    sum_own = [remote(SUM_OWN, k, own_out.at[k], own_in.at[k], sibling) for k in range(blocks)]
    sum_diag = [remote(SUM_DIAG, k, diag_out.at[k], diag_in.at[k], sibling) for k in range(blocks)]
    sum_across = [remote(SUM_ACROSS, k, across_out.at[k], across_in.at[k], partner) for k in range(blocks)]

    ids = seg_row[...].astype(F32)
    eye = lax.broadcasted_iota(jnp.int32, (ROWS, ROWS), 0) == lax.broadcasted_iota(jnp.int32, (ROWS, ROWS), 1)
    id_columns = [
        jnp.sum(jnp.where(eye, ids[:, ROWS * k : ROWS * k + ROWS], 0.0), axis=1, keepdims=True) for k in range(blocks)
    ]
    row_ids = lax.broadcasted_iota(jnp.int32, (slots, slots), 0)
    col_ids = lax.broadcasted_iota(jnp.int32, (slots, slots), 1)
    same = (jnp.concatenate(id_columns, axis=0) == ids) & (row_ids <= col_ids)
    key_position = jnp.sum(jnp.where(same, 1.0, 0.0), axis=0, keepdims=True) - 1.0
    chosen_keys = jnp.where(key_position == row_ids.astype(F32), 1.0, 0.0).astype(BF16)
    factors = dot(turned_table[...], chosen_keys)
    factors = factors[:64] + (factors[64:128] + factors[128:])
    key_cos, key_sin = factors[:32], factors[32:]

    swap_i = lax.broadcasted_iota(jnp.int32, (256, 256), 0)
    swap_j = lax.broadcasted_iota(jnp.int32, (256, 256), 1)
    low = lax.rem(swap_j, HEAD_SIZE) < HEAD_SIZE // 2
    swap = jnp.where(low & (swap_i == swap_j + 32), -1.0, jnp.where(~low & (swap_i == swap_j - 32), 1.0, 0.0))
    swap = swap.astype(BF16)

    ones = jnp.ones((HEAD_SIZE, slots), BF16)
    for n in range(KEY_VALUE_HEADS):
        first = keys[64 * n : 64 * n + 32, :].astype(F32)
        second = keys[64 * n + 32 : 64 * n + 64, :].astype(F32)
        turned_keys[n, :32, :] = (first * key_cos - second * key_sin).astype(BF16)
        turned_keys[n, 32:, :] = (second * key_cos + first * key_sin).astype(BF16)
        wide_values[n, :64, :] = values[64 * n : 64 * n + 64, :]
        wide_values[n, 64:, :] = ones

    def attend(k):
        lo, width = k * ROWS, (k + 1) * ROWS
        block = pl.ds(lo, ROWS)
        q_ids = lax.broadcasted_iota(jnp.int32, (ROWS, width), 0) + lo
        k_ids = lax.broadcasted_iota(jnp.int32, (ROWS, width), 1)
        visible = (id_columns[k] == ids[:, :width]) & (k_ids <= q_ids)
        allowed = visible & ((q_ids - k_ids < WINDOW) | (key_position[:, :width] < SINK))
        bias = jnp.where(allowed, 0.0, MASKED)
        position = jnp.sum(jnp.where(visible, 1.0, 0.0), axis=1, keepdims=True) - 1.0
        chosen = jnp.where(position == k_ids.astype(F32), 1.0, 0.0).astype(BF16)
        turns = dot(chosen, table[:width, :])
        turns = (turns[:, :256] + (turns[:, 256:512] + turns[:, 512:])) * HEAD_SIZE**-0.5
        cos_block = jnp.concatenate([turns[:, :128], turns[:, :128]], axis=1)
        sin_block = jnp.concatenate([turns[:, 128:], turns[:, 128:]], axis=1)
        for n in range(KEY_VALUE_HEADS):
            q = queries[block, pl.ds(256 * n, 256)]
            q = (q.astype(F32) * cos_block + dot(q, swap) * sin_block).astype(BF16)
            q = jnp.concatenate([q[:, 64 * h : 64 * h + 64] for h in range(HEAD_GROUP)], axis=0)
            scores = dot(q, turned_keys[n, :, :width])
            scores = scores.reshape(HEAD_GROUP, ROWS, width) + bias[None]
            raised = jnp.exp(scores - jnp.max(scores, axis=-1, keepdims=True))
            raised = raised.reshape(HEAD_GROUP * ROWS, width).astype(BF16)
            result = dot_t(raised, wide_values[n, :, :width])
            result = result[:, :64] / result[:, 64:]
            context[:, 256 * n : 256 * n + 256] = jnp.concatenate(
                [result[ROWS * h : ROWS * h + ROWS] for h in range(HEAD_GROUP)], axis=1
            ).astype(BF16)

    def project(k):
        block = pl.ds(k * ROWS, ROWS)
        for t in range(tiles):
            cols = pl.ds(LANES * t, LANES)
            mixed[block, cols] = (hidden[block, cols].astype(F32) + dot(context[...], ow[t])).astype(BF16)
        numbers = mixed[block, :].astype(F32)
        factor = lax.rsqrt(jnp.mean(numbers * numbers, axis=-1, keepdims=True) + NORM_EPS)
        rows[k, 0] = (numbers * factor * gain[...].reshape(1, numbers.shape[1])).astype(BF16)

    def feed_forward(k, first_slot):
        def upward(t, carry):
            both = rows[k, first_slot : first_slot + 2].reshape(2 * ROWS, rows.shape[3])
            product = dot(both, wgu[t])
            gate, up = product[:, :HIDDEN_TILE], product[:, HIDDEN_TILE:]
            act[t] = (gate / (1.0 + jnp.exp(-gate)) * up).astype(BF16)
            return carry

        lax.fori_loop(0, hidden_tiles, upward, 0)
        for t in range(tiles):
            hid = jnp.concatenate([act[j] for j in range(hidden_tiles)], axis=1)
            part[:, LANES * t : LANES * t + LANES] = dot(hid, wd[t])

    def start_block(k):
        attend(k)
        if k == 0:
            for copy in ow_loads:
                copy.wait()
            for t in range(hidden_tiles):
                cols = pl.ds(HIDDEN_TILE * t, HIDDEN_TILE)
                ffn_loads.append(load(gate_hbm.at[:, cols], wgu.at[t, :, pl.ds(0, HIDDEN_TILE)]))
                ffn_loads.append(load(up_hbm.at[:, cols], wgu.at[t, :, pl.ds(HIDDEN_TILE, HIDDEN_TILE)]))
            for t in range(tiles):
                ffn_loads.append(load(down_hbm.at[:, pl.ds(LANES * t, LANES)], wd.at[t]))
        project(k)
        if k == 0:
            pl.semaphore_wait(barrier, 2)
        to_partner[k].start()
        to_sibling[k].start()

    def own_rows(k):
        to_sibling[k].wait_recv()
        feed_forward(k, 0)
        own[k] = part[:ROWS, :]
        own_out[k] = part[ROWS:, :].astype(BF16)
        sum_own[k].start()

    def other_rows(k):
        to_partner[k].wait_recv()
        forward[k].start()
        forward[k].wait_recv()
        feed_forward(k, 2)
        diag_out[k] = part[ROWS:, :].astype(BF16)
        sum_diag[k].start()
        sum_diag[k].wait_recv()
        across_out[k] = (part[:ROWS, :] + diag_in[k].astype(F32)).astype(BF16)
        sum_across[k].start()

    live = live_ref[0, 0]
    stores = []

    def finish(k):
        sum_own[k].wait_recv()
        sum_across[k].wait_recv()
        block = pl.ds(k * ROWS, ROWS)
        total = own[k] + own_in[k].astype(F32) + across_in[k].astype(F32) + mixed[block, :].astype(F32)
        slot = lax.broadcasted_iota(jnp.int32, total.shape, 0) + k * ROWS
        finished[block, :] = jnp.where(slot < live, total, 0.0).astype(BF16)
        copy = pltpu.make_async_copy(finished.at[block, :], out.at[block, :], store_sem.at[k])
        copy.start()
        stores.append(copy)

    ready = min(3, blocks)
    for k in range(ready):
        start_block(k)
    for copy in ffn_loads:
        copy.wait()
    for k in range(blocks):
        other_rows(k)
        if k + ready < blocks:
            start_block(k + ready)
        if k >= 1:
            own_rows(k - 1)
    own_rows(blocks - 1)
    for k in range(blocks):
        finish(k)
    for k in range(blocks):
        for copy in (to_sibling[k], to_partner[k], forward[k], sum_own[k], sum_diag[k], sum_across[k]):
            copy.wait_send()
    for copy in stores:
        copy.wait()


def copy_kernel(pieces, source, target, sem):
    rows = source.shape[0] // pieces
    copies = []
    for n in range(pieces):
        block = pl.ds(n * rows, rows)
        copies.append(pltpu.make_async_copy(source.at[block, :], target.at[block, :], sem.at[n]))
        copies[-1].start()
    for copy in copies:
        copy.wait()


def on_device(
    hidden_in, queries, projected_keys, projected_values, segment, live_rows, out_weight, norm_gain,
    gate_weight, up_weight, down_weight,
):
    slots, width = hidden_in.shape
    units = gate_weight.shape[1]
    blocks, tiles, hidden_tiles = slots // ROWS, width // LANES, units // HIDDEN_TILE
    vmem = pl.BlockSpec(memory_space=pltpu.VMEM)
    hbm = pl.BlockSpec(memory_space=pl.ANY)
    block_bf16 = pltpu.VMEM((blocks, ROWS, width), BF16)
    table, turned_table = rotary_table(slots)
    result = pl.pallas_call(
        functools.partial(kernel, blocks),
        out_shape=jax.ShapeDtypeStruct((slots, width), BF16),
        in_specs=[pl.BlockSpec(memory_space=pltpu.SMEM)] + [vmem] * 7 + [hbm] * 5,
        out_specs=hbm,
        scratch_shapes=[
            pltpu.VMEM((slots, width), BF16),
            pltpu.VMEM((tiles, width, LANES), BF16),
            pltpu.VMEM((hidden_tiles, width, 2 * HIDDEN_TILE), BF16),
            pltpu.VMEM((tiles, units, LANES), BF16),
            pltpu.VMEM((blocks, 4, ROWS, width), BF16),
            pltpu.VMEM((ROWS, width), BF16),
            pltpu.VMEM((KEY_VALUE_HEADS, HEAD_SIZE, slots), BF16),
            pltpu.VMEM((KEY_VALUE_HEADS, 2 * HEAD_SIZE, slots), BF16),
            pltpu.VMEM((slots, width), BF16),
            pltpu.VMEM((slots, width), BF16),
            pltpu.VMEM((hidden_tiles, 2 * ROWS, HIDDEN_TILE), BF16),
            pltpu.VMEM((2 * ROWS, width), F32),
            pltpu.VMEM((blocks, ROWS, width), F32),
            block_bf16, block_bf16, block_bf16, block_bf16, block_bf16, block_bf16,
            pltpu.SemaphoreType.DMA((2 * tiles + 2 * hidden_tiles + 1,)),
            pltpu.SemaphoreType.DMA((6, blocks)),
            pltpu.SemaphoreType.DMA((6, blocks)),
            pltpu.SemaphoreType.DMA((blocks,)),
        ],
        compiler_params=pltpu.CompilerParams(
            collective_id=0, has_side_effects=True, vmem_limit_bytes=56 * 1024 * 1024
        ),
        name="decoder_layer",
    )(
        live_rows,
        queries,
        projected_keys.T,
        projected_values.T,
        segment.reshape(1, slots),
        jnp.asarray(table),
        jnp.asarray(turned_table),
        norm_gain,
        hidden_in,
        out_weight,
        gate_weight,
        up_weight,
        down_weight,
    )
    pieces = 8
    return pl.pallas_call(
        functools.partial(copy_kernel, pieces),
        out_shape=jax.ShapeDtypeStruct((slots, width), BF16),
        in_specs=[hbm],
        out_specs=hbm,
        scratch_shapes=[pltpu.SemaphoreType.DMA((pieces,))],
        name="place_result",
    )(result)


def solution(mesh):
    placed = (
        P(("req", "grp"), None),
        P(("req", "grp"), None),
        P(("req", "grp"), None),
        P(("req", "grp"), None),
        P("req", "grp", None),
        P("req", "grp"),
        P(),
        P(),
        P(None, "grp"),
        P(None, "grp"),
        P("grp", None),
    )
    return jax.shard_map(
        on_device, mesh=mesh, in_specs=placed, out_specs=P(("req", "grp"), None), check_vma=False
    )
```

```python
import functools

import jax
import jax.numpy as jnp
import numpy as np
from jax import lax
from jax.experimental import pallas as pl
from jax.experimental.pallas import tpu as pltpu
from jax.sharding import PartitionSpec as P

QUERY_HEADS = 20
KEY_VALUE_HEADS = 5
HEAD_SIZE = 64
WINDOW = 128
SINK = 4
ROPE_BASE = 10000.0
NORM_EPS = 1e-05

MESH = pl.DeviceIdType.MESH
F32 = jnp.float32
BF16 = jnp.bfloat16
ROWS = 128
LANES = 256
HEAD_GROUP = QUERY_HEADS // KEY_VALUE_HEADS
HIDDEN_TILE = 128
MASKED = -1e30

CORE, ACROSS, FORWARD, SUM_OWN, SUM_DIAG, SUM_ACROSS = range(6)


def rotary_table(slot_capacity):
    half = HEAD_SIZE // 2
    inverse = np.float32(ROPE_BASE) ** (-(2.0 * np.arange(half, dtype=np.float32)) / HEAD_SIZE)
    angle = np.arange(slot_capacity, dtype=np.float32)[:, None] * inverse.astype(np.float32)[None, :]
    cosine = np.tile(np.cos(angle.astype(np.float64)), (1, 4))
    sine = np.tile(np.sin(angle.astype(np.float64)), (1, 4))
    exact = np.concatenate([cosine, sine], axis=1).astype(np.float32)
    terms = []
    for _ in range(3):
        term = exact.astype(jnp.bfloat16)
        terms.append(term)
        exact = exact - term.astype(np.float32)
    turned = np.concatenate([np.concatenate([term[:, :half], term[:, 128 : 128 + half]], axis=1).T for term in terms])
    return np.concatenate(terms, axis=1), turned


def dot(a, b):
    return jnp.dot(a, b, preferred_element_type=F32)


def dot_t(a, b):
    return lax.dot_general(a, b, (((1,), (1,)), ((), ())), preferred_element_type=F32)


def kernel(
    blocks,
    live_ref, queries, keys, values, seg_row, table, turned_table, gain, hidden_hbm, ow_hbm, gate_hbm, up_hbm, down_hbm,
    out,
    hidden, ow, wgu, wd, rows, context, turned_keys, wide_values, mixed, finished, act, part, own, across,
    own_out, own_in, diag_out, diag_in, across_out, across_in,
    load_sem, send_sem, recv_sem, store_sem,
):
    me = lax.axis_index("grp")
    sibling = me + 1 - 2 * lax.rem(me, 2)
    partner = lax.rem(me + 2, 4)
    slots = blocks * ROWS
    tiles = ow.shape[0]
    hidden_tiles = wgu.shape[0]

    loads = []

    def load(src, dst):
        copy = pltpu.make_async_copy(src, dst, load_sem.at[len(loads)])
        copy.start()
        loads.append(copy)
        return copy

    ow_loads = [load(ow_hbm.at[:, pl.ds(LANES * t, LANES)], ow.at[t]) for t in range(tiles)]
    ow_loads.append(load(hidden_hbm, hidden))
    ffn_loads = []

    barrier = pltpu.get_barrier_semaphore()
    for other in (sibling, partner):
        pl.semaphore_signal(barrier, inc=1, device_id={"grp": other}, device_id_type=MESH)

    def remote(kind, k, src, dst, other):
        return pltpu.make_async_remote_copy(
            src_ref=src, dst_ref=dst, send_sem=send_sem.at[kind, k], recv_sem=recv_sem.at[kind, k],
            device_id={"grp": other}, device_id_type=MESH,
        )

    to_sibling = [remote(CORE, k, rows.at[k, 0], rows.at[k, 1], sibling) for k in range(blocks)]
    to_partner = [remote(ACROSS, k, rows.at[k, 0], rows.at[k, 2], partner) for k in range(blocks)]
    forward = [remote(FORWARD, k, rows.at[k, 2], rows.at[k, 3], sibling) for k in range(blocks)]
    sum_own = [remote(SUM_OWN, k, own_out.at[k], own_in.at[k], sibling) for k in range(blocks)]
    sum_diag = [remote(SUM_DIAG, k, diag_out.at[k], diag_in.at[k], sibling) for k in range(blocks)]
    sum_across = [remote(SUM_ACROSS, k, across_out.at[k], across_in.at[k], partner) for k in range(blocks)]

    ids = seg_row[...].astype(F32)
    eye = lax.broadcasted_iota(jnp.int32, (ROWS, ROWS), 0) == lax.broadcasted_iota(jnp.int32, (ROWS, ROWS), 1)
    id_columns = [
        jnp.sum(jnp.where(eye, ids[:, ROWS * k : ROWS * k + ROWS], 0.0), axis=1, keepdims=True) for k in range(blocks)
    ]
    row_ids = lax.broadcasted_iota(jnp.int32, (slots, slots), 0)
    col_ids = lax.broadcasted_iota(jnp.int32, (slots, slots), 1)
    same = (jnp.concatenate(id_columns, axis=0) == ids) & (row_ids <= col_ids)
    key_position = jnp.sum(jnp.where(same, 1.0, 0.0), axis=0, keepdims=True) - 1.0
    chosen_keys = jnp.where(key_position == row_ids.astype(F32), 1.0, 0.0).astype(BF16)
    factors = dot(turned_table[...], chosen_keys)
    factors = factors[:64] + (factors[64:128] + factors[128:])
    key_cos, key_sin = factors[:32], factors[32:]

    swap_i = lax.broadcasted_iota(jnp.int32, (256, 256), 0)
    swap_j = lax.broadcasted_iota(jnp.int32, (256, 256), 1)
    low = lax.rem(swap_j, HEAD_SIZE) < HEAD_SIZE // 2
    swap = jnp.where(low & (swap_i == swap_j + 32), -1.0, jnp.where(~low & (swap_i == swap_j - 32), 1.0, 0.0))
    swap = swap.astype(BF16)

    ones = jnp.ones((HEAD_SIZE, slots), BF16)
    for n in range(KEY_VALUE_HEADS):
        first = keys[64 * n : 64 * n + 32, :].astype(F32)
        second = keys[64 * n + 32 : 64 * n + 64, :].astype(F32)
        turned_keys[n, :32, :] = (first * key_cos - second * key_sin).astype(BF16)
        turned_keys[n, 32:, :] = (second * key_cos + first * key_sin).astype(BF16)
        wide_values[n, :64, :] = values[64 * n : 64 * n + 64, :]
        wide_values[n, 64:, :] = ones

    def attend(k):
        lo, width = k * ROWS, (k + 1) * ROWS
        block = pl.ds(lo, ROWS)
        q_ids = lax.broadcasted_iota(jnp.int32, (ROWS, width), 0) + lo
        k_ids = lax.broadcasted_iota(jnp.int32, (ROWS, width), 1)
        visible = (id_columns[k] == ids[:, :width]) & (k_ids <= q_ids)
        allowed = visible & ((q_ids - k_ids < WINDOW) | (key_position[:, :width] < SINK))
        bias = jnp.where(allowed, 0.0, MASKED)
        position = jnp.sum(jnp.where(visible, 1.0, 0.0), axis=1, keepdims=True) - 1.0
        chosen = jnp.where(position == k_ids.astype(F32), 1.0, 0.0).astype(BF16)
        turns = dot(chosen, table[:width, :])
        turns = (turns[:, :256] + (turns[:, 256:512] + turns[:, 512:])) * HEAD_SIZE**-0.5
        cos_block = jnp.concatenate([turns[:, :128], turns[:, :128]], axis=1)
        sin_block = jnp.concatenate([turns[:, 128:], turns[:, 128:]], axis=1)
        for n in range(KEY_VALUE_HEADS):
            q = queries[block, pl.ds(256 * n, 256)]
            q = (q.astype(F32) * cos_block + dot(q, swap) * sin_block).astype(BF16)
            q = jnp.concatenate([q[:, 64 * h : 64 * h + 64] for h in range(HEAD_GROUP)], axis=0)
            scores = dot(q, turned_keys[n, :, :width])
            scores = scores.reshape(HEAD_GROUP, ROWS, width) + bias[None]
            raised = jnp.exp(scores - jnp.max(scores, axis=-1, keepdims=True))
            raised = raised.reshape(HEAD_GROUP * ROWS, width).astype(BF16)
            result = dot_t(raised, wide_values[n, :, :width])
            result = result[:, :64] / result[:, 64:]
            context[:, 256 * n : 256 * n + 256] = jnp.concatenate(
                [result[ROWS * h : ROWS * h + ROWS] for h in range(HEAD_GROUP)], axis=1
            ).astype(BF16)

    def project(k):
        block = pl.ds(k * ROWS, ROWS)
        for t in range(tiles):
            cols = pl.ds(LANES * t, LANES)
            mixed[block, cols] = (hidden[block, cols].astype(F32) + dot(context[...], ow[t])).astype(BF16)
        numbers = mixed[block, :].astype(F32)
        factor = lax.rsqrt(jnp.mean(numbers * numbers, axis=-1, keepdims=True) + NORM_EPS)
        rows[k, 0] = (numbers * factor * gain[...].reshape(1, numbers.shape[1])).astype(BF16)

    def feed_forward(k, first_slot):
        def upward(t, carry):
            both = rows[k, first_slot : first_slot + 2].reshape(2 * ROWS, rows.shape[3])
            product = dot(both, wgu[t])
            gate, up = product[:, :HIDDEN_TILE], product[:, HIDDEN_TILE:]
            act[t] = (gate / (1.0 + jnp.exp(-gate)) * up).astype(BF16)
            return carry

        lax.fori_loop(0, hidden_tiles, upward, 0)
        for t in range(tiles):
            hid = jnp.concatenate([act[j] for j in range(hidden_tiles)], axis=1)
            part[:, LANES * t : LANES * t + LANES] = dot(hid, wd[t])

    def start_block(k):
        attend(k)
        if k == 0:
            for copy in ow_loads:
                copy.wait()
            for t in range(hidden_tiles):
                cols = pl.ds(HIDDEN_TILE * t, HIDDEN_TILE)
                ffn_loads.append(load(gate_hbm.at[:, cols], wgu.at[t, :, pl.ds(0, HIDDEN_TILE)]))
                ffn_loads.append(load(up_hbm.at[:, cols], wgu.at[t, :, pl.ds(HIDDEN_TILE, HIDDEN_TILE)]))
            for t in range(tiles):
                ffn_loads.append(load(down_hbm.at[:, pl.ds(LANES * t, LANES)], wd.at[t]))
        project(k)
        if k == 0:
            pl.semaphore_wait(barrier, 2)
        to_partner[k].start()
        to_sibling[k].start()

    def own_rows(k):
        to_sibling[k].wait_recv()
        feed_forward(k, 0)
        own[k] = part[:ROWS, :]
        own_out[k] = part[ROWS:, :].astype(BF16)
        sum_own[k].start()

    def pass_on(k):
        to_partner[k].wait_recv()
        forward[k].start()

    def other_rows(k):
        forward[k].wait_recv()
        feed_forward(k, 2)
        diag_out[k] = part[ROWS:, :].astype(BF16)
        sum_diag[k].start()
        across[k] = part[:ROWS, :]

    def send_across(k):
        sum_diag[k].wait_recv()
        across_out[k] = (across[k] + diag_in[k].astype(F32)).astype(BF16)
        sum_across[k].start()

    live = live_ref[0, 0]
    stores = []

    def finish(k):
        sum_own[k].wait_recv()
        sum_across[k].wait_recv()
        block = pl.ds(k * ROWS, ROWS)
        total = own[k] + own_in[k].astype(F32) + across_in[k].astype(F32) + mixed[block, :].astype(F32)
        slot = lax.broadcasted_iota(jnp.int32, total.shape, 0) + k * ROWS
        finished[block, :] = jnp.where(slot < live, total, 0.0).astype(BF16)
        copy = pltpu.make_async_copy(finished.at[block, :], out.at[block, :], store_sem.at[k])
        copy.start()
        stores.append(copy)

    ready = min(3, blocks)
    for k in range(ready):
        start_block(k)
    pass_on(0)
    for k in range(ready, blocks):
        start_block(k)
    for copy in ffn_loads:
        copy.wait()
    for k in range(blocks):
        other_rows(k)
        if k + 1 < blocks:
            pass_on(k + 1)
            own_rows(k)
            send_across(k)
    send_across(blocks - 1)
    own_rows(blocks - 1)
    for k in range(blocks):
        finish(k)
    for k in range(blocks):
        for copy in (to_sibling[k], to_partner[k], forward[k], sum_own[k], sum_diag[k], sum_across[k]):
            copy.wait_send()
    for copy in stores:
        copy.wait()


def copy_kernel(pieces, source, target, held, load_sem, store_sem):
    rows = source.shape[0] // pieces
    loads, stores = [], []
    for n in range(pieces):
        block = pl.ds(n * rows, rows)
        loads.append(pltpu.make_async_copy(source.at[block, :], held.at[block, :], load_sem.at[n]))
        stores.append(pltpu.make_async_copy(held.at[block, :], target.at[block, :], store_sem.at[n]))
        loads[-1].start()
    for load, store in zip(loads, stores):
        load.wait()
        store.start()
    for store in stores:
        store.wait()


def on_device(
    hidden_in, queries, projected_keys, projected_values, segment, live_rows, out_weight, norm_gain,
    gate_weight, up_weight, down_weight,
):
    slots, width = hidden_in.shape
    units = gate_weight.shape[1]
    blocks, tiles, hidden_tiles = slots // ROWS, width // LANES, units // HIDDEN_TILE
    vmem = pl.BlockSpec(memory_space=pltpu.VMEM)
    hbm = pl.BlockSpec(memory_space=pl.ANY)
    block_bf16 = pltpu.VMEM((blocks, ROWS, width), BF16)
    table, turned_table = rotary_table(slots)
    result = pl.pallas_call(
        functools.partial(kernel, blocks),
        out_shape=jax.ShapeDtypeStruct((slots, width), BF16),
        in_specs=[pl.BlockSpec(memory_space=pltpu.SMEM)] + [vmem] * 7 + [hbm] * 5,
        out_specs=hbm,
        scratch_shapes=[
            pltpu.VMEM((slots, width), BF16),
            pltpu.VMEM((tiles, width, LANES), BF16),
            pltpu.VMEM((hidden_tiles, width, 2 * HIDDEN_TILE), BF16),
            pltpu.VMEM((tiles, units, LANES), BF16),
            pltpu.VMEM((blocks, 4, ROWS, width), BF16),
            pltpu.VMEM((ROWS, width), BF16),
            pltpu.VMEM((KEY_VALUE_HEADS, HEAD_SIZE, slots), BF16),
            pltpu.VMEM((KEY_VALUE_HEADS, 2 * HEAD_SIZE, slots), BF16),
            pltpu.VMEM((slots, width), BF16),
            pltpu.VMEM((slots, width), BF16),
            pltpu.VMEM((hidden_tiles, 2 * ROWS, HIDDEN_TILE), BF16),
            pltpu.VMEM((2 * ROWS, width), F32),
            pltpu.VMEM((blocks, ROWS, width), F32),
            pltpu.VMEM((blocks, ROWS, width), F32),
            block_bf16, block_bf16, block_bf16, block_bf16, block_bf16, block_bf16,
            pltpu.SemaphoreType.DMA((2 * tiles + 2 * hidden_tiles + 1,)),
            pltpu.SemaphoreType.DMA((6, blocks)),
            pltpu.SemaphoreType.DMA((6, blocks)),
            pltpu.SemaphoreType.DMA((blocks,)),
        ],
        compiler_params=pltpu.CompilerParams(
            collective_id=0, has_side_effects=True, vmem_limit_bytes=56 * 1024 * 1024
        ),
        name="decoder_layer",
    )(
        live_rows,
        queries,
        projected_keys.T,
        projected_values.T,
        segment.reshape(1, slots),
        jnp.asarray(table),
        jnp.asarray(turned_table),
        norm_gain,
        hidden_in,
        out_weight,
        gate_weight,
        up_weight,
        down_weight,
    )
    pieces = 8
    return pl.pallas_call(
        functools.partial(copy_kernel, pieces),
        out_shape=jax.ShapeDtypeStruct((slots, width), BF16),
        in_specs=[hbm],
        out_specs=hbm,
        scratch_shapes=[
            pltpu.VMEM((slots, width), BF16),
            pltpu.SemaphoreType.DMA((pieces,)),
            pltpu.SemaphoreType.DMA((pieces,)),
        ],
        name="place_result",
    )(result)


def solution(mesh):
    placed = (
        P(("req", "grp"), None),
        P(("req", "grp"), None),
        P(("req", "grp"), None),
        P(("req", "grp"), None),
        P("req", "grp", None),
        P("req", "grp"),
        P(),
        P(),
        P(None, "grp"),
        P(None, "grp"),
        P("grp", None),
    )
    return jax.shard_map(
        on_device, mesh=mesh, in_specs=placed, out_specs=P(("req", "grp"), None), check_vma=False
    )
```

```python
import functools

import jax
import jax.numpy as jnp
import numpy as np
from jax import lax
from jax.experimental import pallas as pl
from jax.experimental.pallas import tpu as pltpu
from jax.sharding import PartitionSpec as P

QUERY_HEADS = 20
KEY_VALUE_HEADS = 5
HEAD_SIZE = 64
WINDOW = 128
SINK = 4
ROPE_BASE = 10000.0
NORM_EPS = 1e-05

MESH = pl.DeviceIdType.MESH
F32 = jnp.float32
BF16 = jnp.bfloat16
ROWS = 128
LANES = 256
HEAD_GROUP = QUERY_HEADS // KEY_VALUE_HEADS
HIDDEN_TILE = 128
MASKED = -1e30

CORE, ACROSS, FORWARD, SUM_OWN, SUM_DIAG, SUM_ACROSS = range(6)


def rotary_table(slot_capacity):
    half = HEAD_SIZE // 2
    inverse = np.float32(ROPE_BASE) ** (-(2.0 * np.arange(half, dtype=np.float32)) / HEAD_SIZE)
    angle = np.arange(slot_capacity, dtype=np.float32)[:, None] * inverse.astype(np.float32)[None, :]
    cosine = np.tile(np.cos(angle.astype(np.float64)), (1, 4))
    sine = np.tile(np.sin(angle.astype(np.float64)), (1, 4))
    exact = np.concatenate([cosine, sine], axis=1).astype(np.float32)
    terms = []
    for _ in range(3):
        term = exact.astype(jnp.bfloat16)
        terms.append(term)
        exact = exact - term.astype(np.float32)
    turned = np.concatenate([np.concatenate([term[:, :half], term[:, 128 : 128 + half]], axis=1).T for term in terms])
    return np.concatenate(terms, axis=1), turned


def dot(a, b):
    return jnp.dot(a, b, preferred_element_type=F32)


def dot_t(a, b):
    return lax.dot_general(a, b, (((1,), (1,)), ((), ())), preferred_element_type=F32)


def kernel(
    blocks,
    live_ref, queries, keys, values, seg_row, table, turned_table, gain, hidden_hbm, ow_hbm, gate_hbm, up_hbm, down_hbm,
    out,
    hidden, ow, wgu, wd, rows, context, turned_keys, wide_values, mixed, finished, act, part, own, across,
    own_out, own_in, diag_out, diag_in, across_out, across_in,
    load_sem, send_sem, recv_sem, store_sem,
):
    me = lax.axis_index("grp")
    sibling = me + 1 - 2 * lax.rem(me, 2)
    partner = lax.rem(me + 2, 4)
    slots = blocks * ROWS
    tiles = ow.shape[0]
    hidden_tiles = wgu.shape[0]

    loads = []

    def load(src, dst):
        copy = pltpu.make_async_copy(src, dst, load_sem.at[len(loads)])
        copy.start()
        loads.append(copy)
        return copy

    ow_loads = [load(ow_hbm.at[:, pl.ds(LANES * t, LANES)], ow.at[t]) for t in range(tiles)]
    ow_loads.append(load(hidden_hbm, hidden))
    ffn_loads = []

    barrier = pltpu.get_barrier_semaphore()
    for other in (sibling, partner):
        pl.semaphore_signal(barrier, inc=1, device_id={"grp": other}, device_id_type=MESH)

    def remote(kind, k, src, dst, other):
        return pltpu.make_async_remote_copy(
            src_ref=src, dst_ref=dst, send_sem=send_sem.at[kind, k], recv_sem=recv_sem.at[kind, k],
            device_id={"grp": other}, device_id_type=MESH,
        )

    to_sibling = [remote(CORE, k, rows.at[k, 0], rows.at[k, 1], sibling) for k in range(blocks)]
    to_partner = [remote(ACROSS, k, rows.at[k, 0], rows.at[k, 2], partner) for k in range(blocks)]
    forward = [remote(FORWARD, k, rows.at[k, 2], rows.at[k, 3], sibling) for k in range(blocks)]
    sum_own = [remote(SUM_OWN, k, own_out.at[k], own_in.at[k], sibling) for k in range(blocks)]
    sum_diag = [remote(SUM_DIAG, k, diag_out.at[k], diag_in.at[k], sibling) for k in range(blocks)]
    sum_across = [remote(SUM_ACROSS, k, across_out.at[k], across_in.at[k], partner) for k in range(blocks)]

    ids = seg_row[...].astype(F32)
    eye = lax.broadcasted_iota(jnp.int32, (ROWS, ROWS), 0) == lax.broadcasted_iota(jnp.int32, (ROWS, ROWS), 1)
    id_columns = [
        jnp.sum(jnp.where(eye, ids[:, ROWS * k : ROWS * k + ROWS], 0.0), axis=1, keepdims=True) for k in range(blocks)
    ]
    swap_i = lax.broadcasted_iota(jnp.int32, (256, 256), 0)
    swap_j = lax.broadcasted_iota(jnp.int32, (256, 256), 1)
    low = lax.rem(swap_j, HEAD_SIZE) < HEAD_SIZE // 2
    swap = jnp.where(low & (swap_i == swap_j + 32), -1.0, jnp.where(~low & (swap_i == swap_j - 32), 1.0, 0.0))
    swap = swap.astype(BF16)

    ones = jnp.ones((HEAD_SIZE, ROWS), BF16)
    key_positions = []

    def prepare(k):
        lo, width = k * ROWS, (k + 1) * ROWS
        block = pl.ds(lo, ROWS)
        row_ids = lax.broadcasted_iota(jnp.int32, (width, ROWS), 0)
        col_ids = lax.broadcasted_iota(jnp.int32, (width, ROWS), 1) + lo
        same = (jnp.concatenate(id_columns[: k + 1], axis=0) == ids[:, lo:width]) & (row_ids <= col_ids)
        key_position = jnp.sum(jnp.where(same, 1.0, 0.0), axis=0, keepdims=True) - 1.0
        key_positions.append(key_position)
        chosen_keys = jnp.where(key_position == row_ids.astype(F32), 1.0, 0.0).astype(BF16)
        factors = dot(turned_table[:, :width], chosen_keys)
        factors = factors[:64] + (factors[64:128] + factors[128:])
        key_cos, key_sin = factors[:32], factors[32:]
        for n in range(KEY_VALUE_HEADS):
            first = keys[64 * n : 64 * n + 32, block].astype(F32)
            second = keys[64 * n + 32 : 64 * n + 64, block].astype(F32)
            turned_keys[n, :32, block] = (first * key_cos - second * key_sin).astype(BF16)
            turned_keys[n, 32:, block] = (second * key_cos + first * key_sin).astype(BF16)
            wide_values[n, :64, block] = values[64 * n : 64 * n + 64, block]
            wide_values[n, 64:, block] = ones

    def attend(k):
        lo, width = k * ROWS, (k + 1) * ROWS
        block = pl.ds(lo, ROWS)
        q_ids = lax.broadcasted_iota(jnp.int32, (ROWS, width), 0) + lo
        k_ids = lax.broadcasted_iota(jnp.int32, (ROWS, width), 1)
        key_position = jnp.concatenate(key_positions, axis=1)
        visible = (id_columns[k] == ids[:, :width]) & (k_ids <= q_ids)
        allowed = visible & ((q_ids - k_ids < WINDOW) | (key_position < SINK))
        bias = jnp.where(allowed, 0.0, MASKED)
        position = jnp.sum(jnp.where(visible, 1.0, 0.0), axis=1, keepdims=True) - 1.0
        chosen = jnp.where(position == k_ids.astype(F32), 1.0, 0.0).astype(BF16)
        turns = dot(chosen, table[:width, :])
        turns = (turns[:, :256] + (turns[:, 256:512] + turns[:, 512:])) * HEAD_SIZE**-0.5
        cos_block = jnp.concatenate([turns[:, :128], turns[:, :128]], axis=1)
        sin_block = jnp.concatenate([turns[:, 128:], turns[:, 128:]], axis=1)
        for n in range(KEY_VALUE_HEADS):
            q = queries[block, pl.ds(256 * n, 256)]
            q = (q.astype(F32) * cos_block + dot(q, swap) * sin_block).astype(BF16)
            q = jnp.concatenate([q[:, 64 * h : 64 * h + 64] for h in range(HEAD_GROUP)], axis=0)
            scores = dot(q, turned_keys[n, :, :width])
            scores = scores.reshape(HEAD_GROUP, ROWS, width) + bias[None]
            raised = jnp.exp(scores - jnp.max(scores, axis=-1, keepdims=True))
            raised = raised.reshape(HEAD_GROUP * ROWS, width).astype(BF16)
            result = dot_t(raised, wide_values[n, :, :width])
            result = result[:, :64] / result[:, 64:]
            context[:, 256 * n : 256 * n + 256] = jnp.concatenate(
                [result[ROWS * h : ROWS * h + ROWS] for h in range(HEAD_GROUP)], axis=1
            ).astype(BF16)

    def project(k):
        block = pl.ds(k * ROWS, ROWS)
        for t in range(tiles):
            cols = pl.ds(LANES * t, LANES)
            mixed[block, cols] = (hidden[block, cols].astype(F32) + dot(context[...], ow[t])).astype(BF16)
        numbers = mixed[block, :].astype(F32)
        factor = lax.rsqrt(jnp.mean(numbers * numbers, axis=-1, keepdims=True) + NORM_EPS)
        rows[k, 0] = (numbers * factor * gain[...].reshape(1, numbers.shape[1])).astype(BF16)

    def feed_forward(k, first_slot):
        def upward(t, carry):
            both = rows[k, first_slot : first_slot + 2].reshape(2 * ROWS, rows.shape[3])
            product = dot(both, wgu[t])
            gate, up = product[:, :HIDDEN_TILE], product[:, HIDDEN_TILE:]
            act[t] = (gate / (1.0 + jnp.exp(-gate)) * up).astype(BF16)
            return carry

        lax.fori_loop(0, hidden_tiles, upward, 0)
        for t in range(tiles):
            hid = jnp.concatenate([act[j] for j in range(hidden_tiles)], axis=1)
            part[:, LANES * t : LANES * t + LANES] = dot(hid, wd[t])

    def start_block(k):
        prepare(k)
        attend(k)
        if k == 0:
            for copy in ow_loads:
                copy.wait()
            for t in range(hidden_tiles):
                cols = pl.ds(HIDDEN_TILE * t, HIDDEN_TILE)
                ffn_loads.append(load(gate_hbm.at[:, cols], wgu.at[t, :, pl.ds(0, HIDDEN_TILE)]))
                ffn_loads.append(load(up_hbm.at[:, cols], wgu.at[t, :, pl.ds(HIDDEN_TILE, HIDDEN_TILE)]))
            for t in range(tiles):
                ffn_loads.append(load(down_hbm.at[:, pl.ds(LANES * t, LANES)], wd.at[t]))
        project(k)
        if k == 0:
            pl.semaphore_wait(barrier, 2)
        to_partner[k].start()
        to_sibling[k].start()

    def own_rows(k):
        to_sibling[k].wait_recv()
        feed_forward(k, 0)
        own[k] = part[:ROWS, :]
        own_out[k] = part[ROWS:, :].astype(BF16)
        sum_own[k].start()

    def pass_on(k):
        to_partner[k].wait_recv()
        forward[k].start()

    def other_rows(k):
        forward[k].wait_recv()
        feed_forward(k, 2)
        diag_out[k] = part[ROWS:, :].astype(BF16)
        sum_diag[k].start()
        across[k] = part[:ROWS, :]

    def send_across(k):
        sum_diag[k].wait_recv()
        across_out[k] = (across[k] + diag_in[k].astype(F32)).astype(BF16)
        sum_across[k].start()

    live = live_ref[0, 0]
    stores = []

    def finish(k):
        sum_own[k].wait_recv()
        sum_across[k].wait_recv()
        block = pl.ds(k * ROWS, ROWS)
        total = own[k] + own_in[k].astype(F32) + across_in[k].astype(F32) + mixed[block, :].astype(F32)
        slot = lax.broadcasted_iota(jnp.int32, total.shape, 0) + k * ROWS
        finished[block, :] = jnp.where(slot < live, total, 0.0).astype(BF16)
        copy = pltpu.make_async_copy(finished.at[block, :], out.at[block, :], store_sem.at[k])
        copy.start()
        stores.append(copy)

    ready = min(3, blocks)
    for k in range(ready):
        start_block(k)
    pass_on(0)
    for k in range(ready, blocks):
        start_block(k)
    for copy in ffn_loads:
        copy.wait()
    for k in range(blocks):
        other_rows(k)
        if k + 1 < blocks:
            pass_on(k + 1)
        if k >= 1:
            send_across(k - 1)
    own_rows(0)
    send_across(blocks - 1)
    for k in range(1, blocks):
        own_rows(k)
    for k in range(blocks):
        finish(k)
    for k in range(blocks):
        for copy in (to_sibling[k], to_partner[k], forward[k], sum_own[k], sum_diag[k], sum_across[k]):
            copy.wait_send()
    for copy in stores:
        copy.wait()


def copy_kernel(pieces, source, target, held, load_sem, store_sem):
    rows = source.shape[0] // pieces
    loads, stores = [], []
    for n in range(pieces):
        block = pl.ds(n * rows, rows)
        loads.append(pltpu.make_async_copy(source.at[block, :], held.at[block, :], load_sem.at[n]))
        stores.append(pltpu.make_async_copy(held.at[block, :], target.at[block, :], store_sem.at[n]))
        loads[-1].start()
    for load, store in zip(loads, stores):
        load.wait()
        store.start()
    for store in stores:
        store.wait()


def on_device(
    hidden_in, queries, projected_keys, projected_values, segment, live_rows, out_weight, norm_gain,
    gate_weight, up_weight, down_weight,
):
    slots, width = hidden_in.shape
    units = gate_weight.shape[1]
    blocks, tiles, hidden_tiles = slots // ROWS, width // LANES, units // HIDDEN_TILE
    vmem = pl.BlockSpec(memory_space=pltpu.VMEM)
    hbm = pl.BlockSpec(memory_space=pl.ANY)
    block_bf16 = pltpu.VMEM((blocks, ROWS, width), BF16)
    table, turned_table = rotary_table(slots)
    result = pl.pallas_call(
        functools.partial(kernel, blocks),
        out_shape=jax.ShapeDtypeStruct((slots, width), BF16),
        in_specs=[pl.BlockSpec(memory_space=pltpu.SMEM)] + [vmem] * 7 + [hbm] * 5,
        out_specs=hbm,
        scratch_shapes=[
            pltpu.VMEM((slots, width), BF16),
            pltpu.VMEM((tiles, width, LANES), BF16),
            pltpu.VMEM((hidden_tiles, width, 2 * HIDDEN_TILE), BF16),
            pltpu.VMEM((tiles, units, LANES), BF16),
            pltpu.VMEM((blocks, 4, ROWS, width), BF16),
            pltpu.VMEM((ROWS, width), BF16),
            pltpu.VMEM((KEY_VALUE_HEADS, HEAD_SIZE, slots), BF16),
            pltpu.VMEM((KEY_VALUE_HEADS, 2 * HEAD_SIZE, slots), BF16),
            pltpu.VMEM((slots, width), BF16),
            pltpu.VMEM((slots, width), BF16),
            pltpu.VMEM((hidden_tiles, 2 * ROWS, HIDDEN_TILE), BF16),
            pltpu.VMEM((2 * ROWS, width), F32),
            pltpu.VMEM((blocks, ROWS, width), F32),
            pltpu.VMEM((blocks, ROWS, width), F32),
            block_bf16, block_bf16, block_bf16, block_bf16, block_bf16, block_bf16,
            pltpu.SemaphoreType.DMA((2 * tiles + 2 * hidden_tiles + 1,)),
            pltpu.SemaphoreType.DMA((6, blocks)),
            pltpu.SemaphoreType.DMA((6, blocks)),
            pltpu.SemaphoreType.DMA((blocks,)),
        ],
        compiler_params=pltpu.CompilerParams(
            collective_id=0, has_side_effects=True, vmem_limit_bytes=56 * 1024 * 1024
        ),
        name="decoder_layer",
    )(
        live_rows,
        queries,
        projected_keys.T,
        projected_values.T,
        segment.reshape(1, slots),
        jnp.asarray(table),
        jnp.asarray(turned_table),
        norm_gain,
        hidden_in,
        out_weight,
        gate_weight,
        up_weight,
        down_weight,
    )
    pieces = 8
    return pl.pallas_call(
        functools.partial(copy_kernel, pieces),
        out_shape=jax.ShapeDtypeStruct((slots, width), BF16),
        in_specs=[hbm],
        out_specs=hbm,
        scratch_shapes=[
            pltpu.VMEM((slots, width), BF16),
            pltpu.SemaphoreType.DMA((pieces,)),
            pltpu.SemaphoreType.DMA((pieces,)),
        ],
        name="place_result",
    )(result)


def solution(mesh):
    placed = (
        P(("req", "grp"), None),
        P(("req", "grp"), None),
        P(("req", "grp"), None),
        P(("req", "grp"), None),
        P("req", "grp", None),
        P("req", "grp"),
        P(),
        P(),
        P(None, "grp"),
        P(None, "grp"),
        P("grp", None),
    )
    return jax.shard_map(
        on_device, mesh=mesh, in_specs=placed, out_specs=P(("req", "grp"), None), check_vma=False
    )
```

```python
import functools

import jax
import jax.numpy as jnp
import numpy as np
from jax import lax
from jax.experimental import pallas as pl
from jax.experimental.pallas import tpu as pltpu
from jax.sharding import PartitionSpec as P

QUERY_HEADS = 20
KEY_VALUE_HEADS = 5
HEAD_SIZE = 64
WINDOW = 128
SINK = 4
ROPE_BASE = 10000.0
NORM_EPS = 1e-05

MESH = pl.DeviceIdType.MESH
F32 = jnp.float32
BF16 = jnp.bfloat16
ROWS = 128
LANES = 256
HEAD_GROUP = QUERY_HEADS // KEY_VALUE_HEADS
HIDDEN_TILE = 128
MASKED = -1e30

CORE, ACROSS, FORWARD, SUM_OWN, SUM_DIAG, SUM_ACROSS = range(6)


def rotary_table(slot_capacity):
    half = HEAD_SIZE // 2
    inverse = np.float32(ROPE_BASE) ** (-(2.0 * np.arange(half, dtype=np.float32)) / HEAD_SIZE)
    angle = np.arange(slot_capacity, dtype=np.float32)[:, None] * inverse.astype(np.float32)[None, :]
    cosine = np.tile(np.cos(angle.astype(np.float64)), (1, 4))
    sine = np.tile(np.sin(angle.astype(np.float64)), (1, 4))
    exact = np.concatenate([cosine, sine], axis=1).astype(np.float32)
    terms = []
    for _ in range(3):
        term = exact.astype(jnp.bfloat16)
        terms.append(term)
        exact = exact - term.astype(np.float32)
    turned = np.concatenate([np.concatenate([term[:, :half], term[:, 128 : 128 + half]], axis=1).T for term in terms])
    return np.concatenate(terms, axis=1), turned


def dot(a, b):
    return jnp.dot(a, b, preferred_element_type=F32)


def dot_t(a, b):
    return lax.dot_general(a, b, (((1,), (1,)), ((), ())), preferred_element_type=F32)


def kernel(
    blocks,
    live_ref, queries, keys, values, seg_row, table, turned_table, gain, hidden_hbm, ow_hbm, gate_hbm, up_hbm, down_hbm,
    out,
    hidden, ow, wgu, wd, rows, context, turned_keys, wide_values, mixed, finished, act, part, own, across,
    own_out, own_in, diag_out, diag_in, across_out, across_in,
    load_sem, send_sem, recv_sem, store_sem,
):
    me = lax.axis_index("grp")
    sibling = me + 1 - 2 * lax.rem(me, 2)
    partner = lax.rem(me + 2, 4)
    slots = blocks * ROWS
    tiles = ow.shape[0]
    hidden_tiles = wgu.shape[0]

    loads = []

    def load(src, dst):
        copy = pltpu.make_async_copy(src, dst, load_sem.at[len(loads)])
        copy.start()
        loads.append(copy)
        return copy

    ow_loads = [load(ow_hbm.at[:, pl.ds(LANES * t, LANES)], ow.at[t]) for t in range(tiles)]
    ow_loads.append(load(hidden_hbm, hidden))
    ffn_loads = []

    barrier = pltpu.get_barrier_semaphore()
    for other in (sibling, partner):
        pl.semaphore_signal(barrier, inc=1, device_id={"grp": other}, device_id_type=MESH)

    def remote(kind, k, src, dst, other):
        return pltpu.make_async_remote_copy(
            src_ref=src, dst_ref=dst, send_sem=send_sem.at[kind, k], recv_sem=recv_sem.at[kind, k],
            device_id={"grp": other}, device_id_type=MESH,
        )

    to_sibling = [remote(CORE, k, rows.at[k, 0], rows.at[k, 1], sibling) for k in range(blocks)]
    to_partner = [remote(ACROSS, k, rows.at[k, 0], rows.at[k, 2], partner) for k in range(blocks)]
    forward = [remote(FORWARD, k, rows.at[k, 2], rows.at[k, 3], sibling) for k in range(blocks)]
    sum_own = [remote(SUM_OWN, k, own_out.at[k], own_in.at[k], sibling) for k in range(blocks)]
    sum_diag = [remote(SUM_DIAG, k, diag_out.at[k], diag_in.at[k], sibling) for k in range(blocks)]
    sum_across = [remote(SUM_ACROSS, k, across_out.at[k], across_in.at[k], partner) for k in range(blocks)]

    ids = seg_row[...].astype(F32)
    eye = lax.broadcasted_iota(jnp.int32, (ROWS, ROWS), 0) == lax.broadcasted_iota(jnp.int32, (ROWS, ROWS), 1)
    id_columns = [
        jnp.sum(jnp.where(eye, ids[:, ROWS * k : ROWS * k + ROWS], 0.0), axis=1, keepdims=True) for k in range(blocks)
    ]
    swap_i = lax.broadcasted_iota(jnp.int32, (256, 256), 0)
    swap_j = lax.broadcasted_iota(jnp.int32, (256, 256), 1)
    low = lax.rem(swap_j, HEAD_SIZE) < HEAD_SIZE // 2
    swap = jnp.where(low & (swap_i == swap_j + 32), -1.0, jnp.where(~low & (swap_i == swap_j - 32), 1.0, 0.0))
    swap = swap.astype(BF16)

    ones = jnp.ones((HEAD_SIZE, ROWS), BF16)
    key_positions = []

    def prepare(k):
        lo, width = k * ROWS, (k + 1) * ROWS
        block = pl.ds(lo, ROWS)
        row_ids = lax.broadcasted_iota(jnp.int32, (width, ROWS), 0)
        col_ids = lax.broadcasted_iota(jnp.int32, (width, ROWS), 1) + lo
        same = (jnp.concatenate(id_columns[: k + 1], axis=0) == ids[:, lo:width]) & (row_ids <= col_ids)
        key_position = jnp.sum(jnp.where(same, 1.0, 0.0), axis=0, keepdims=True) - 1.0
        key_positions.append(key_position)
        chosen_keys = jnp.where(key_position == row_ids.astype(F32), 1.0, 0.0).astype(BF16)
        factors = dot(turned_table[:, :width], chosen_keys)
        factors = factors[:64] + (factors[64:128] + factors[128:])
        key_cos, key_sin = factors[:32], factors[32:]
        for n in range(KEY_VALUE_HEADS):
            first = keys[64 * n : 64 * n + 32, block].astype(F32)
            second = keys[64 * n + 32 : 64 * n + 64, block].astype(F32)
            turned_keys[n, :32, block] = (first * key_cos - second * key_sin).astype(BF16)
            turned_keys[n, 32:, block] = (second * key_cos + first * key_sin).astype(BF16)
            wide_values[n, :64, block] = values[64 * n : 64 * n + 64, block]
            wide_values[n, 64:, block] = ones

    def attend(k):
        lo, width = k * ROWS, (k + 1) * ROWS
        block = pl.ds(lo, ROWS)
        q_ids = lax.broadcasted_iota(jnp.int32, (ROWS, width), 0) + lo
        k_ids = lax.broadcasted_iota(jnp.int32, (ROWS, width), 1)
        key_position = jnp.concatenate(key_positions, axis=1)
        visible = (id_columns[k] == ids[:, :width]) & (k_ids <= q_ids)
        allowed = visible & ((q_ids - k_ids < WINDOW) | (key_position < SINK))
        bias = jnp.where(allowed, 0.0, MASKED)
        position = jnp.sum(jnp.where(visible, 1.0, 0.0), axis=1, keepdims=True) - 1.0
        chosen = jnp.where(position == k_ids.astype(F32), 1.0, 0.0).astype(BF16)
        turns = dot(chosen, table[:width, :])
        turns = (turns[:, :256] + (turns[:, 256:512] + turns[:, 512:])) * HEAD_SIZE**-0.5
        cos_block = jnp.concatenate([turns[:, :128], turns[:, :128]], axis=1)
        sin_block = jnp.concatenate([turns[:, 128:], turns[:, 128:]], axis=1)
        for n in range(KEY_VALUE_HEADS):
            q = queries[block, pl.ds(256 * n, 256)]
            q = (q.astype(F32) * cos_block + dot(q, swap) * sin_block).astype(BF16)
            q = jnp.concatenate([q[:, 64 * h : 64 * h + 64] for h in range(HEAD_GROUP)], axis=0)
            scores = dot(q, turned_keys[n, :, :width])
            scores = scores.reshape(HEAD_GROUP, ROWS, width) + bias[None]
            raised = jnp.exp(scores - jnp.max(scores, axis=-1, keepdims=True))
            raised = raised.reshape(HEAD_GROUP * ROWS, width).astype(BF16)
            result = dot_t(raised, wide_values[n, :, :width])
            result = result[:, :64] / result[:, 64:]
            context[:, 256 * n : 256 * n + 256] = jnp.concatenate(
                [result[ROWS * h : ROWS * h + ROWS] for h in range(HEAD_GROUP)], axis=1
            ).astype(BF16)

    def project(k):
        block = pl.ds(k * ROWS, ROWS)
        for t in range(tiles):
            cols = pl.ds(LANES * t, LANES)
            mixed[block, cols] = (hidden[block, cols].astype(F32) + dot(context[...], ow[t])).astype(BF16)
        numbers = mixed[block, :].astype(F32)
        factor = lax.rsqrt(jnp.mean(numbers * numbers, axis=-1, keepdims=True) + NORM_EPS)
        rows[k, 0] = (numbers * factor * gain[...].reshape(1, numbers.shape[1])).astype(BF16)

    def feed_forward(k, first_slot):
        def upward(t, carry):
            both = rows[k : k + 2, first_slot : first_slot + 2].reshape(4 * ROWS, rows.shape[3])
            product = dot(both, wgu[t])
            gate, up = product[:, :HIDDEN_TILE], product[:, HIDDEN_TILE:]
            act[t] = (gate / (1.0 + jnp.exp(-gate)) * up).astype(BF16)
            return carry

        lax.fori_loop(0, hidden_tiles, upward, 0, unroll=True)
        for t in range(tiles):
            hid = jnp.concatenate([act[j] for j in range(hidden_tiles)], axis=1)
            part[:, LANES * t : LANES * t + LANES] = dot(hid, wd[t])

    def start_block(k):
        prepare(k)
        attend(k)
        if k == 0:
            for copy in ow_loads:
                copy.wait()
            for t in range(hidden_tiles):
                cols = pl.ds(HIDDEN_TILE * t, HIDDEN_TILE)
                ffn_loads.append(load(gate_hbm.at[:, cols], wgu.at[t, :, pl.ds(0, HIDDEN_TILE)]))
                ffn_loads.append(load(up_hbm.at[:, cols], wgu.at[t, :, pl.ds(HIDDEN_TILE, HIDDEN_TILE)]))
            for t in range(tiles):
                ffn_loads.append(load(down_hbm.at[:, pl.ds(LANES * t, LANES)], wd.at[t]))
        project(k)
        if k == 0:
            pl.semaphore_wait(barrier, 2)
        to_partner[k].start()
        to_sibling[k].start()

    def own_rows(pair):
        for k in pair:
            to_sibling[k].wait_recv()
        feed_forward(pair[0], 0)
        for j, k in enumerate(pair):
            own[k] = part[2 * j * ROWS : (2 * j + 1) * ROWS, :]
            own_out[k] = part[(2 * j + 1) * ROWS : (2 * j + 2) * ROWS, :].astype(BF16)
            sum_own[k].start()

    def pass_on(k):
        to_partner[k].wait_recv()
        forward[k].start()

    def other_rows(pair):
        for k in pair:
            forward[k].wait_recv()
        feed_forward(pair[0], 2)
        for j, k in enumerate(pair):
            diag_out[k] = part[(2 * j + 1) * ROWS : (2 * j + 2) * ROWS, :].astype(BF16)
            sum_diag[k].start()
            across[k] = part[2 * j * ROWS : (2 * j + 1) * ROWS, :]

    def send_across(k):
        sum_diag[k].wait_recv()
        across_out[k] = (across[k] + diag_in[k].astype(F32)).astype(BF16)
        sum_across[k].start()

    live = live_ref[0, 0]
    stores = []

    def finish(k):
        sum_own[k].wait_recv()
        sum_across[k].wait_recv()
        block = pl.ds(k * ROWS, ROWS)
        total = own[k] + own_in[k].astype(F32) + across_in[k].astype(F32) + mixed[block, :].astype(F32)
        slot = lax.broadcasted_iota(jnp.int32, total.shape, 0) + k * ROWS
        finished[block, :] = jnp.where(slot < live, total, 0.0).astype(BF16)
        copy = pltpu.make_async_copy(finished.at[block, :], out.at[block, :], store_sem.at[k])
        copy.start()
        stores.append(copy)

    for k in range(blocks - 1):
        start_block(k)
    pass_on(0)
    start_block(blocks - 1)
    pass_on(1)
    for copy in ffn_loads:
        copy.wait()
    for first in range(0, blocks, 2):
        pair = (first, first + 1)
        other_rows(pair)
        if first + 2 < blocks:
            pass_on(first + 2)
        for k in pair:
            send_across(k)
        if first + 2 < blocks:
            own_rows(pair)
            pass_on(first + 3)
    own_rows((blocks - 2, blocks - 1))
    for k in range(blocks):
        finish(k)
    for k in range(blocks):
        for copy in (to_sibling[k], to_partner[k], forward[k], sum_own[k], sum_diag[k], sum_across[k]):
            copy.wait_send()
    for copy in stores:
        copy.wait()


def copy_kernel(pieces, source, target, held, load_sem, store_sem):
    rows = source.shape[0] // pieces
    loads, stores = [], []
    for n in range(pieces):
        block = pl.ds(n * rows, rows)
        loads.append(pltpu.make_async_copy(source.at[block, :], held.at[block, :], load_sem.at[n]))
        stores.append(pltpu.make_async_copy(held.at[block, :], target.at[block, :], store_sem.at[n]))
        loads[-1].start()
    for load, store in zip(loads, stores):
        load.wait()
        store.start()
    for store in stores:
        store.wait()


def on_device(
    hidden_in, queries, projected_keys, projected_values, segment, live_rows, out_weight, norm_gain,
    gate_weight, up_weight, down_weight,
):
    slots, width = hidden_in.shape
    units = gate_weight.shape[1]
    blocks, tiles, hidden_tiles = slots // ROWS, width // LANES, units // HIDDEN_TILE
    vmem = pl.BlockSpec(memory_space=pltpu.VMEM)
    hbm = pl.BlockSpec(memory_space=pl.ANY)
    block_bf16 = pltpu.VMEM((blocks, ROWS, width), BF16)
    table, turned_table = rotary_table(slots)
    result = pl.pallas_call(
        functools.partial(kernel, blocks),
        out_shape=jax.ShapeDtypeStruct((slots, width), BF16),
        in_specs=[pl.BlockSpec(memory_space=pltpu.SMEM)] + [vmem] * 7 + [hbm] * 5,
        out_specs=hbm,
        scratch_shapes=[
            pltpu.VMEM((slots, width), BF16),
            pltpu.VMEM((tiles, width, LANES), BF16),
            pltpu.VMEM((hidden_tiles, width, 2 * HIDDEN_TILE), BF16),
            pltpu.VMEM((tiles, units, LANES), BF16),
            pltpu.VMEM((blocks, 4, ROWS, width), BF16),
            pltpu.VMEM((ROWS, width), BF16),
            pltpu.VMEM((KEY_VALUE_HEADS, HEAD_SIZE, slots), BF16),
            pltpu.VMEM((KEY_VALUE_HEADS, 2 * HEAD_SIZE, slots), BF16),
            pltpu.VMEM((slots, width), BF16),
            pltpu.VMEM((slots, width), BF16),
            pltpu.VMEM((hidden_tiles, 4 * ROWS, HIDDEN_TILE), BF16),
            pltpu.VMEM((4 * ROWS, width), F32),
            pltpu.VMEM((blocks, ROWS, width), F32),
            pltpu.VMEM((blocks, ROWS, width), F32),
            block_bf16, block_bf16, block_bf16, block_bf16, block_bf16, block_bf16,
            pltpu.SemaphoreType.DMA((2 * tiles + 2 * hidden_tiles + 1,)),
            pltpu.SemaphoreType.DMA((6, blocks)),
            pltpu.SemaphoreType.DMA((6, blocks)),
            pltpu.SemaphoreType.DMA((blocks,)),
        ],
        compiler_params=pltpu.CompilerParams(
            collective_id=0, has_side_effects=True, vmem_limit_bytes=56 * 1024 * 1024
        ),
        name="decoder_layer",
    )(
        live_rows,
        queries,
        projected_keys.T,
        projected_values.T,
        segment.reshape(1, slots),
        jnp.asarray(table),
        jnp.asarray(turned_table),
        norm_gain,
        hidden_in,
        out_weight,
        gate_weight,
        up_weight,
        down_weight,
    )
    pieces = 8
    return pl.pallas_call(
        functools.partial(copy_kernel, pieces),
        out_shape=jax.ShapeDtypeStruct((slots, width), BF16),
        in_specs=[hbm],
        out_specs=hbm,
        scratch_shapes=[
            pltpu.VMEM((slots, width), BF16),
            pltpu.SemaphoreType.DMA((pieces,)),
            pltpu.SemaphoreType.DMA((pieces,)),
        ],
        name="place_result",
    )(result)


def solution(mesh):
    placed = (
        P(("req", "grp"), None),
        P(("req", "grp"), None),
        P(("req", "grp"), None),
        P(("req", "grp"), None),
        P("req", "grp", None),
        P("req", "grp"),
        P(),
        P(),
        P(None, "grp"),
        P(None, "grp"),
        P("grp", None),
    )
    return jax.shard_map(
        on_device, mesh=mesh, in_specs=placed, out_specs=P(("req", "grp"), None), check_vma=False
    )
```
